32 devices in a mesh: vocab: 8 (over z, y), tok: 4 (over x, core).
Axes of the slice: x: 2, y: 2, z: 4, core: 2. Of those that a mesh axis runs over, the one named last changes fastest.
Arguments:
- teacher_hidden: bfloat16 [512, 8192], P(None, 'tok'), may hold values from -80 to 80
- teacher_head: bfloat16 [8192, 81920], P('tok', 'vocab'), may hold values from -0.0625 to 0.0625
- student_hidden: bfloat16 [512, 3584], replicated, may hold values from -80 to 80
- student_head: bfloat16 [3584, 81920], P(None, ('vocab', 'tok')), may hold values from -0.09375 to 0.09375
- grammar_bits: int32 [512, 5120], P('tok', 'vocab'), may hold values from 0 to 65535
- sampled_ids: int32 [512], replicated, may hold values from 0 to 81919
Outputs:
- distill_loss: float32 [], replicated
- head_grad: bfloat16 [3584, 81920], P(None, ('vocab', 'tok'))
- hidden_grad: float32 [512, 3584], P(('vocab', 'tok'))
The draws below stay inside these ranges and needn't reach their ends.
All inputs are finite; a program needn't handle non-finite values.
Results may differ from the reference program's by a relative error of at most 0.0038.
Values may be sent and summed in bfloat16 or wider, within the bound.
A program may use at most 192 MiB of HBM per device.

```python
import jax
import jax.numpy as jnp
from jax import lax

DT = 8192
DS = 3584
V = 81920
TOKENS = 512


def scaled_rows(key, row_total, width):
    base = jnp.clip(jax.random.normal(key, (row_total, width), jnp.float32), -4.0, 4.0)
    return (3.0 * base).astype(jnp.bfloat16)


def draw_teacher_hidden(key, part):
    return scaled_rows(jax.random.fold_in(key, 11), TOKENS, DT)


def draw_student_hidden(key, part):
    return scaled_rows(jax.random.fold_in(key, 23), TOKENS, DS)


def place_ends(values, stream_key, low, top_value):
    index_at = [jax.random.randint(jax.random.fold_in(stream_key, axis), (), 0, length) for axis, length in enumerate(values.shape)]
    main_axis = values.shape.index(max(values.shape))
    next_to = index_at[:main_axis] + [(index_at[main_axis] + 1) % values.shape[main_axis]] + index_at[main_axis + 1:]
    return values.at[tuple(index_at)].set(low).at[tuple(next_to)].set(top_value)


def shard_levels(own_key, shape, cuts, low, top_value):
    def one(axis_at, shards_of):
        heights = jax.random.uniform(jax.random.fold_in(jax.random.fold_in(own_key, 6), axis_at), (shards_of,), jnp.float32, low / len(cuts), top_value / len(cuts))
        return jnp.repeat(jnp.exp(heights), shape[axis_at] // shards_of).reshape((-1,) + (1,) * (len(shape) - axis_at - 1))

    loudness = one(*cuts[0])
    for cut in cuts[1:]:
        loudness = loudness * one(*cut)
    return loudness


def centred(stream_key, dims, scale, most, shards=(), kind=jnp.bfloat16):
    values = scale * jax.random.normal(stream_key, dims, jnp.float32)
    if shards:
        values = values * shard_levels(stream_key, dims, shards, -0.22, 0.18)
    return jnp.clip(values, -most, most).astype(kind)


def setup_inputs(seed: int = 0) -> dict:
    keys = jax.random.split(jax.random.key(seed), 7)
    return {
        "teacher_hidden": draw_teacher_hidden(jax.random.fold_in(keys[6], 71), 0),
        "teacher_head": centred(keys[1], (DT, V), DT ** -0.5, 0.0625, ((0, 4), (1, 8))),
        "student_hidden": draw_student_hidden(jax.random.fold_in(keys[6], 71), 0),
        "student_head": centred(keys[3], (DS, V), DS ** -0.5, 0.09375, ((1, 32),)),
        "grammar_bits": place_ends(jax.random.randint(keys[4], (TOKENS, V // 16), 0, 65536), jax.random.fold_in(keys[4], 1), 0, 65535).astype(jnp.int32),
        "sampled_ids": place_ends(jax.random.randint(keys[5], (TOKENS,), 0, V), jax.random.fold_in(keys[5], 1), 0, V - 1).astype(jnp.int32),
    }


sample_weight = 0.5


def admitted(packed, sampled_ids, column_start):
    shifts = jnp.arange(16, dtype=jnp.int32)
    bit_values = jnp.right_shift(packed[:, :, None], shifts[None, None, :]) & 1
    unpacked = bit_values.reshape(packed.shape[0], packed.shape[1] * 16)
    columns = column_start + jnp.arange(unpacked.shape[1], dtype=jnp.int32)
    chosen = columns[None, :] == sampled_ids[:, None]
    return (unpacked == 1) | chosen, chosen


def masked_stats(logits, allowed):
    masked = jnp.where(allowed, logits, -1e30)
    local_max = jnp.max(masked, axis=1)
    local_sum = jnp.sum(jnp.where(allowed, jnp.exp(masked - local_max[:, None]), 0.0), axis=1)
    return local_max, local_sum


def reference(teacher_hidden, teacher_head, student_hidden, student_head, grammar_bits, sampled_ids):
    teacher_logit = jnp.dot(teacher_hidden, teacher_head, preferred_element_type=jnp.float32)
    allowed, chosen = admitted(grammar_bits, sampled_ids, 0)
    teacher_max, teacher_sum = masked_stats(teacher_logit, allowed)
    shifted = teacher_logit - teacher_max[:, None]
    teacher_prob = jnp.where(allowed, jnp.exp(shifted) / teacher_sum[:, None], 0.0).astype(jnp.bfloat16)
    teacher_log = shifted - jnp.log(teacher_sum)[:, None]
    student_logit = jnp.dot(student_hidden, student_head, preferred_element_type=jnp.float32)
    student_max = jnp.max(student_logit, axis=1)
    student_sum = jnp.sum(jnp.exp(student_logit - student_max[:, None]), axis=1)
    student_log = student_logit - student_max[:, None] - jnp.log(student_sum)[:, None]
    prob_wide = teacher_prob.astype(jnp.float32)
    divergence = jnp.sum(jnp.where(allowed, prob_wide * teacher_log, 0.0)) - jnp.sum(prob_wide * student_log)
    picked = jnp.sum(jnp.where(chosen, student_log - teacher_log, 0.0))
    distill_loss = (divergence + sample_weight * picked) / TOKENS
    logit_grad = ((1.0 - sample_weight) * jnp.exp(student_log) - prob_wide
                  + sample_weight * chosen.astype(jnp.float32)).astype(jnp.bfloat16)
    head_grad = lax.dot_general(student_hidden, logit_grad, (((0,), (0,)), ((), ())),
                                preferred_element_type=jnp.float32).astype(jnp.bfloat16)
    hidden_grad = lax.dot_general(logit_grad, student_head, (((1,), (1,)), ((), ())),
                                  preferred_element_type=jnp.float32)
    return (distill_loss, head_grad, hidden_grad)
```

```python
import functools

import jax
import jax.numpy as jnp
from jax import lax
from jax.experimental import pallas as pl
from jax.experimental.pallas import tpu as pltpu
from jax.sharding import PartitionSpec as P

sample_weight = 0.5
grad_scale = 4096.0
MESH = pl.DeviceIdType.MESH


def bits_of(size):
    return size.bit_length() - 1


def swapped(value, axis, bit):
    size = lax.axis_size(axis)
    return lax.ppermute(value, axis, [(i, i ^ (1 << bit)) for i in range(size)])


def chunk_kernel(first_ref, a_ref, b_ref, *rest):
    out_ref = rest[-1]
    total = jnp.dot(a_ref[...], b_ref[...], preferred_element_type=jnp.float32)
    for extra in rest[:-1]:
        total = total + extra[...].astype(jnp.float32)
    out_ref[...] = total.astype(out_ref.dtype)


def chunk_product(a, b, first, width, tile, out_dtype, extras=()):
    rows, depth = a.shape
    tiles = width // tile
    grid_spec = pltpu.PrefetchScalarGridSpec(
        num_scalar_prefetch=1,
        grid=(tiles,),
        in_specs=[
            pl.BlockSpec((rows, depth), lambda i, f: (0, 0)),
            pl.BlockSpec((depth, tile), lambda i, f: (0, f[0] + i)),
        ]
        + [pl.BlockSpec((rows, tile), lambda i, f: (0, i)) for _ in extras],
        out_specs=pl.BlockSpec((rows, tile), lambda i, f: (0, i)),
    )
    return pl.pallas_call(
        chunk_kernel,
        grid_spec=grid_spec,
        out_shape=jax.ShapeDtypeStruct((rows, width), out_dtype),
        compiler_params=pltpu.CompilerParams(vmem_limit_bytes=40 * 1024 * 1024),
        cost_estimate=pl.CostEstimate(
            flops=2 * rows * depth * width,
            bytes_accessed=2 * (rows * depth + depth * width + 2 * rows * width),
            transcendentals=0,
        ),
    )((first // tile).reshape(1).astype(jnp.int32), a, b, *extras)


def grad_kernel(hidden_ref, grad_ref, *rest):
    rest[-1][...] = lax.dot_general(
        hidden_ref[...],
        grad_ref[...],
        (((0,), (0,)), ((), ())),
        preferred_element_type=jnp.float32,
    ).astype(jnp.bfloat16)


def grad_rows(hidden, grad, earlier, step, tile):
    tokens, width = hidden.shape
    columns = grad.shape[1]
    cut = 2 if columns % 256 == 0 else 1
    held = () if earlier is None else (earlier,)
    return pl.pallas_call(
        grad_kernel,
        grid=(cut,),
        in_specs=[
            pl.BlockSpec((tokens, tile), lambda i: (0, step)),
            pl.BlockSpec((tokens, columns // cut), lambda i: (0, i)),
        ]
        + [pl.BlockSpec(memory_space=pl.ANY) for _ in held],
        out_specs=pl.BlockSpec((tile, columns // cut), lambda i: (step, i)),
        out_shape=jax.ShapeDtypeStruct((width, columns), jnp.bfloat16),
        input_output_aliases={2: 0} if held else {},
        compiler_params=pltpu.CompilerParams(vmem_limit_bytes=24 * 1024 * 1024),
        cost_estimate=pl.CostEstimate(
            flops=2 * tokens * tile * columns,
            bytes_accessed=2 * (tokens * tile + tokens * columns + tile * columns),
            transcendentals=0,
        ),
    )(hidden, grad, *held)


def merge_rows(parts):
    teacher_top = jnp.max(parts[:, 0, :], axis=0, keepdims=True)
    student_top = jnp.max(parts[:, 3, :], axis=0, keepdims=True)
    teacher_shift = parts[:, 0, :] - teacher_top
    student_shift = parts[:, 3, :] - student_top
    scale = jnp.exp(teacher_shift)
    teacher_sum = jnp.sum(parts[:, 1, :] * scale, axis=0, keepdims=True)
    cross = jnp.sum(
        scale * (parts[:, 2, :] + parts[:, 1, :] * (teacher_shift - student_shift)),
        axis=0,
        keepdims=True,
    )
    student_sum = jnp.sum(parts[:, 4, :] * jnp.exp(student_shift), axis=0, keepdims=True)
    picked = jnp.sum(parts[:, 5, :], axis=0, keepdims=True)
    return jnp.concatenate(
        [teacher_top, teacher_sum, cross, student_top, student_sum, picked, picked, picked], axis=0
    )


def stats_kernel(
    groups, ways, part_ref, out_ref, tok_ref, vocab_ref, send_a, recv_a, send_b, recv_b
):
    mine = lax.axis_index("tok")
    place = lax.axis_index("vocab")
    barrier = pltpu.get_barrier_semaphore()
    for step in range(1, groups):
        pl.semaphore_signal(
            barrier,
            inc=1,
            device_id=(place, lax.rem(mine + step, groups)),
            device_id_type=MESH,
        )
    for step in range(1, ways):
        pl.semaphore_signal(
            barrier,
            inc=1,
            device_id=(lax.rem(place + step, ways), mine),
            device_id_type=MESH,
        )
    pl.semaphore_wait(barrier, groups + ways - 2)
    tok_ref[0] = part_ref[...]
    copies = []
    for step in range(1, groups):
        copy = pltpu.make_async_remote_copy(
            src_ref=part_ref,
            dst_ref=tok_ref.at[step],
            send_sem=send_a.at[step],
            recv_sem=recv_a.at[step],
            device_id=(place, lax.rem(mine + step, groups)),
            device_id_type=MESH,
        )
        copy.start()
        copies.append(copy)
    for copy in copies:
        copy.wait()
    vocab_ref[0] = merge_rows(tok_ref[...])
    copies = []
    for step in range(1, ways):
        copy = pltpu.make_async_remote_copy(
            src_ref=vocab_ref.at[0],
            dst_ref=vocab_ref.at[step],
            send_sem=send_b.at[step],
            recv_sem=recv_b.at[step],
            device_id=(lax.rem(place + step, ways), mine),
            device_id_type=MESH,
        )
        copy.start()
        copies.append(copy)
    for copy in copies:
        copy.wait()
    out_ref[...] = merge_rows(vocab_ref[...])


def merged_stats(part):
    groups = lax.axis_size("tok")
    ways = lax.axis_size("vocab")
    return pl.pallas_call(
        functools.partial(stats_kernel, groups, ways),
        out_shape=jax.ShapeDtypeStruct(part.shape, jnp.float32),
        in_specs=[pl.BlockSpec(memory_space=pltpu.VMEM)],
        out_specs=pl.BlockSpec(memory_space=pltpu.VMEM),
        scratch_shapes=[
            pltpu.VMEM((groups,) + part.shape, jnp.float32),
            pltpu.VMEM((ways,) + part.shape, jnp.float32),
            pltpu.SemaphoreType.DMA((groups,)),
            pltpu.SemaphoreType.DMA((groups,)),
            pltpu.SemaphoreType.DMA((ways,)),
            pltpu.SemaphoreType.DMA((ways,)),
        ],
        compiler_params=pltpu.CompilerParams(collective_id=0, has_side_effects=True),
    )(part)


def words_here(grammar_bits, width):
    groups = lax.axis_size("tok")
    mine = lax.axis_index("tok")
    pieces = grammar_bits.reshape(grammar_bits.shape[0], groups, width)
    got = [lax.dynamic_index_in_dim(pieces, mine, 1, False)]
    for step in range(1, groups):
        piece = lax.dynamic_index_in_dim(pieces, mine ^ step, 1, False)
        got.append(lax.ppermute(piece, "tok", [(i, i ^ step) for i in range(groups)]))
    stacked = jnp.stack(got)
    return jnp.concatenate(
        [lax.dynamic_index_in_dim(stacked, mine ^ block, 0, False) for block in range(groups)]
    )


def admitted(words, columns):
    width = words.shape[1]
    low = (words & 255).astype(jnp.bfloat16)
    high = jnp.right_shift(words, 8).astype(jnp.bfloat16)
    spread = jnp.arange(columns, dtype=jnp.int32)
    sources = jnp.arange(2 * width, dtype=jnp.int32)
    wanted = spread // 16 + jnp.where(spread % 16 >= 8, width, 0)
    picks = (sources[:, None] == wanted[None, :]).astype(jnp.bfloat16)
    octets = jnp.dot(
        jnp.concatenate([low, high], axis=1), picks, preferred_element_type=jnp.float32
    ).astype(jnp.int32)
    return jnp.right_shift(octets, (spread % 8)[None, :]) & 1


def split_rows(value):
    groups, ways = lax.axis_size("tok"), lax.axis_size("vocab")
    left = [("vocab", b) for b in reversed(range(bits_of(ways)))]
    left += [("tok", b) for b in reversed(range(bits_of(groups)))]
    rows = value.shape[0] // (groups * ways)
    return left, value.reshape((2,) * len(left) + (rows, value.shape[1]))


def halves_of(total, left, key):
    at = left.index(key)
    bit = (lax.axis_index(key[0]) >> key[1]) & 1
    away = lax.dynamic_index_in_dim(total, 1 - bit, at, False).astype(jnp.float16)
    return away, lax.dynamic_index_in_dim(total, bit, at, False).astype(jnp.float32)


def per_device(
    teacher_hidden, teacher_head, student_hidden, student_head, grammar_bits, sampled_ids
):
    groups = lax.axis_size("tok")
    mine = lax.axis_index("tok")
    place = lax.axis_index("vocab")
    token_total = student_hidden.shape[0]
    columns = student_head.shape[1]
    start = (place * groups + mine) * columns
    tile = 256
    half = columns // 2

    def product(target, lower, dtype, extras=()):
        return chunk_product(
            teacher_hidden, teacher_head, target * columns + lower, half, tile, dtype, extras
        )

    far, near = [], []
    for lower in (0, half):
        away = product(mine ^ 3, lower, jnp.float32)
        far.append(swapped(away, "tok", 0))
    sent = []
    for at, lower in enumerate((0, half)):
        away = product(mine ^ 2, lower, jnp.float32, (far[at],))
        sent.append(swapped(away.astype(jnp.float16), "tok", 1))
    for lower in (0, half):
        away = product(mine ^ 1, lower, jnp.float32)
        near.append(swapped(away, "tok", 0))
    own = [product(mine, lower, jnp.float32, (near[at],)) for at, lower in enumerate((0, half))]

    student_logit = jnp.dot(student_hidden, student_head, preferred_element_type=jnp.float32)
    student_top = jnp.max(student_logit, axis=1)
    student_sum = jnp.sum(jnp.exp(student_logit - student_top[:, None]), axis=1)
    bit = admitted(words_here(grammar_bits, columns // 16), columns)
    here = start + jnp.arange(columns, dtype=jnp.int32)
    chosen = here[None, :] == sampled_ids[:, None]
    penalty = jnp.where((bit == 1) | chosen, 0.0, -1e30).astype(jnp.bfloat16)

    teacher_logit = jnp.concatenate(
        [own[at] + sent[at].astype(jnp.float32) for at in range(2)], axis=1
    )
    masked = jnp.where(penalty < 0, -1e30, teacher_logit)
    top = jnp.max(masked, axis=1)
    shifted = masked - top[:, None]
    weight = jnp.where(penalty < 0, 0.0, jnp.exp(shifted))
    weight_sum = jnp.sum(weight, axis=1)
    cross = jnp.sum(
        jnp.where(
            penalty < 0, 0.0, weight * (shifted - (student_logit - student_top[:, None]))
        ),
        axis=1,
    )
    picked = jnp.sum(jnp.where(chosen, student_logit - masked, 0.0), axis=1)
    zero = jnp.zeros_like(top)
    part = jnp.stack([top, weight_sum, cross, student_top, student_sum, picked, zero, zero])
    merged = merged_stats(part)
    teacher_top, teacher_sum, cross, student_top, student_sum, picked = (
        merged[i] for i in range(6)
    )
    teacher_lse = jnp.log(teacher_sum)
    student_lse = jnp.log(student_sum)
    divergence = cross / teacher_sum - teacher_lse + student_lse
    gap = picked + (teacher_top - student_top) + (teacher_lse - student_lse)
    distill_loss = jnp.sum(divergence + sample_weight * gap) / token_total

    prob = jnp.where(
        penalty < 0, 0.0, jnp.exp(masked - teacher_top[:, None]) / teacher_sum[:, None]
    ).astype(jnp.bfloat16)
    student_log = student_logit - student_top[:, None] - student_lse[:, None]
    logit_grad = (
        (1.0 - sample_weight) * jnp.exp(student_log)
        - prob.astype(jnp.float32)
        + sample_weight * chosen.astype(jnp.float32)
    ).astype(jnp.bfloat16)

    tok_bits = [("tok", b) for b in range(bits_of(groups))]
    vocab_bits = [("vocab", b) for b in range(bits_of(lax.axis_size("vocab")))]
    orders = (
        tok_bits + vocab_bits,
        tok_bits[:1] + vocab_bits[:1] + tok_bits[1:] + vocab_bits[1:],
    )
    width = student_head.shape[0] // 2
    blocks = []
    for at in range(2):
        block = lax.dot_general(
            logit_grad,
            lax.slice_in_dim(student_head, at * width, (at + 1) * width, axis=0),
            (((1,), (1,)), ((), ())),
            preferred_element_type=jnp.float32,
        )
        blocks.append(block * grad_scale)
    step_rows = 512 if student_hidden.shape[1] % 512 == 0 else 128
    steps = student_hidden.shape[1] // step_rows
    levels = len(orders[0])
    shares = [2, 3, 1, 1] + [0] * levels
    head_grad = None
    step = 0
    lefts, totals = zip(*[split_rows(block) for block in blocks])
    for level in range(levels):
        aways, keeps = [], []
        for at in range(2):
            away, keep = halves_of(totals[at], lefts[at], orders[at][level])
            aways.append(away)
            keeps.append(keep)
        *aways, logit_grad = lax.optimization_barrier((*aways, logit_grad))
        got = [swapped(aways[at], *orders[at][level]) for at in range(2)]
        until = steps if level == levels - 1 else min(steps, step + shares[level])
        if until > step:
            while step < until:
                head_grad = grad_rows(student_hidden, logit_grad, head_grad, step, step_rows)
                step += 1
            *got, head_grad = lax.optimization_barrier((*got, head_grad))
        totals = [keeps[at] + got[at].astype(jnp.float32) for at in range(2)]
        for at in range(2):
            lefts[at].remove(orders[at][level])
    hidden_grad = jnp.concatenate(totals, axis=1) * (1.0 / grad_scale)
    return (distill_loss, head_grad, hidden_grad)


def solution(mesh):
    placed = (
        P(None, "tok"),
        P("tok", "vocab"),
        P(),
        P(None, ("vocab", "tok")),
        P("tok", "vocab"),
        P(),
    )
    return jax.shard_map(
        per_device,
        mesh=mesh,
        in_specs=placed,
        out_specs=(P(), P(None, ("vocab", "tok")), P(("vocab", "tok"), None)),
        check_vma=False,
    )
```

```python
import functools

import jax
import jax.numpy as jnp
from jax import lax
from jax.experimental import pallas as pl
from jax.experimental.pallas import tpu as pltpu
from jax.sharding import PartitionSpec as P

sample_weight = 0.5
grad_scale = 4096.0
MESH = pl.DeviceIdType.MESH


def bits_of(size):
    return size.bit_length() - 1


def swapped(value, axis, bit):
    size = lax.axis_size(axis)
    return lax.ppermute(value, axis, [(i, i ^ (1 << bit)) for i in range(size)])


def chunk_kernel(first_ref, a_ref, b_ref, *rest):
    out_ref = rest[-1]
    total = jnp.dot(a_ref[...], b_ref[...], preferred_element_type=jnp.float32)
    for extra in rest[:-1]:
        total = total + extra[...].astype(jnp.float32)
    out_ref[...] = total.astype(out_ref.dtype)


def chunk_product(a, b, first, width, tile, out_dtype, extras=()):
    rows, depth = a.shape
    tiles = width // tile
    grid_spec = pltpu.PrefetchScalarGridSpec(
        num_scalar_prefetch=1,
        grid=(tiles,),
        in_specs=[
            pl.BlockSpec((rows, depth), lambda i, f: (0, 0)),
            pl.BlockSpec((depth, tile), lambda i, f: (0, f[0] + i)),
        ]
        + [pl.BlockSpec((rows, tile), lambda i, f: (0, i)) for _ in extras],
        out_specs=pl.BlockSpec((rows, tile), lambda i, f: (0, i)),
    )
    return pl.pallas_call(
        chunk_kernel,
        grid_spec=grid_spec,
        out_shape=jax.ShapeDtypeStruct((rows, width), out_dtype),
        compiler_params=pltpu.CompilerParams(vmem_limit_bytes=40 * 1024 * 1024),
        cost_estimate=pl.CostEstimate(
            flops=rows * depth * width // 8,
            bytes_accessed=(rows * depth + depth * width + 2 * rows * width) // 8,
            transcendentals=0,
        ),
    )((first // tile).reshape(1).astype(jnp.int32), a, b, *extras)


def grad_kernel(hidden_ref, grad_ref, *rest):
    rest[-1][...] = lax.dot_general(
        hidden_ref[...],
        grad_ref[...],
        (((0,), (0,)), ((), ())),
        preferred_element_type=jnp.float32,
    ).astype(jnp.bfloat16)


def grad_rows(hidden, grad, earlier, step, tile):
    tokens, width = hidden.shape
    columns = grad.shape[1]
    cut = 2 if columns % 256 == 0 else 1
    held = () if earlier is None else (earlier,)
    return pl.pallas_call(
        grad_kernel,
        grid=(cut,),
        in_specs=[
            pl.BlockSpec((tokens, tile), lambda i: (0, step)),
            pl.BlockSpec((tokens, columns // cut), lambda i: (0, i)),
        ]
        + [pl.BlockSpec(memory_space=pl.ANY) for _ in held],
        out_specs=pl.BlockSpec((tile, columns // cut), lambda i: (step, i)),
        out_shape=jax.ShapeDtypeStruct((width, columns), jnp.bfloat16),
        input_output_aliases={2: 0} if held else {},
        compiler_params=pltpu.CompilerParams(vmem_limit_bytes=24 * 1024 * 1024),
        cost_estimate=pl.CostEstimate(
            flops=2 * tokens * tile * columns,
            bytes_accessed=2 * (tokens * tile + tokens * columns + tile * columns),
            transcendentals=0,
        ),
    )(hidden, grad, *held)


def merge_rows(parts):
    teacher_top = jnp.max(parts[:, 0, :], axis=0, keepdims=True)
    student_top = jnp.max(parts[:, 3, :], axis=0, keepdims=True)
    teacher_shift = parts[:, 0, :] - teacher_top
    student_shift = parts[:, 3, :] - student_top
    scale = jnp.exp(teacher_shift)
    teacher_sum = jnp.sum(parts[:, 1, :] * scale, axis=0, keepdims=True)
    cross = jnp.sum(
        scale * (parts[:, 2, :] + parts[:, 1, :] * (teacher_shift - student_shift)),
        axis=0,
        keepdims=True,
    )
    student_sum = jnp.sum(parts[:, 4, :] * jnp.exp(student_shift), axis=0, keepdims=True)
    picked = jnp.sum(parts[:, 5, :], axis=0, keepdims=True)
    return jnp.concatenate(
        [teacher_top, teacher_sum, cross, student_top, student_sum, picked, picked, picked], axis=0
    )


def stats_kernel(
    groups, ways, part_ref, out_ref, tok_ref, vocab_ref, send_a, recv_a, send_b, recv_b
):
    mine = lax.axis_index("tok")
    place = lax.axis_index("vocab")
    barrier = pltpu.get_barrier_semaphore()
    for step in range(1, groups):
        pl.semaphore_signal(
            barrier,
            inc=1,
            device_id=(place, lax.rem(mine + step, groups)),
            device_id_type=MESH,
        )
    for step in range(1, ways):
        pl.semaphore_signal(
            barrier,
            inc=1,
            device_id=(lax.rem(place + step, ways), mine),
            device_id_type=MESH,
        )
    pl.semaphore_wait(barrier, groups + ways - 2)
    tok_ref[0] = part_ref[...]
    copies = []
    for step in range(1, groups):
        copy = pltpu.make_async_remote_copy(
            src_ref=part_ref,
            dst_ref=tok_ref.at[step],
            send_sem=send_a.at[step],
            recv_sem=recv_a.at[step],
            device_id=(place, lax.rem(mine + step, groups)),
            device_id_type=MESH,
        )
        copy.start()
        copies.append(copy)
    for copy in copies:
        copy.wait()
    vocab_ref[0] = merge_rows(tok_ref[...])
    copies = []
    for step in range(1, ways):
        copy = pltpu.make_async_remote_copy(
            src_ref=vocab_ref.at[0],
            dst_ref=vocab_ref.at[step],
            send_sem=send_b.at[step],
            recv_sem=recv_b.at[step],
            device_id=(lax.rem(place + step, ways), mine),
            device_id_type=MESH,
        )
        copy.start()
        copies.append(copy)
    for copy in copies:
        copy.wait()
    out_ref[...] = merge_rows(vocab_ref[...])


def merged_stats(part):
    groups = lax.axis_size("tok")
    ways = lax.axis_size("vocab")
    return pl.pallas_call(
        functools.partial(stats_kernel, groups, ways),
        out_shape=jax.ShapeDtypeStruct(part.shape, jnp.float32),
        in_specs=[pl.BlockSpec(memory_space=pltpu.VMEM)],
        out_specs=pl.BlockSpec(memory_space=pltpu.VMEM),
        scratch_shapes=[
            pltpu.VMEM((groups,) + part.shape, jnp.float32),
            pltpu.VMEM((ways,) + part.shape, jnp.float32),
            pltpu.SemaphoreType.DMA((groups,)),
            pltpu.SemaphoreType.DMA((groups,)),
            pltpu.SemaphoreType.DMA((ways,)),
            pltpu.SemaphoreType.DMA((ways,)),
        ],
        compiler_params=pltpu.CompilerParams(collective_id=0, has_side_effects=True),
    )(part)


def words_here(grammar_bits, width):
    groups = lax.axis_size("tok")
    mine = lax.axis_index("tok")
    pieces = grammar_bits.reshape(grammar_bits.shape[0], groups, width)
    got = [lax.dynamic_index_in_dim(pieces, mine, 1, False)]
    for step in range(1, groups):
        piece = lax.dynamic_index_in_dim(pieces, mine ^ step, 1, False)
        got.append(lax.ppermute(piece, "tok", [(i, i ^ step) for i in range(groups)]))
    stacked = jnp.stack(got)
    return jnp.concatenate(
        [lax.dynamic_index_in_dim(stacked, mine ^ block, 0, False) for block in range(groups)]
    )


def admitted(words, columns):
    width = words.shape[1]
    low = (words & 255).astype(jnp.bfloat16)
    high = jnp.right_shift(words, 8).astype(jnp.bfloat16)
    spread = jnp.arange(columns, dtype=jnp.int32)
    sources = jnp.arange(2 * width, dtype=jnp.int32)
    wanted = spread // 16 + jnp.where(spread % 16 >= 8, width, 0)
    picks = (sources[:, None] == wanted[None, :]).astype(jnp.bfloat16)
    octets = jnp.dot(
        jnp.concatenate([low, high], axis=1), picks, preferred_element_type=jnp.float32
    ).astype(jnp.int32)
    return jnp.right_shift(octets, (spread % 8)[None, :]) & 1


def split_rows(value):
    groups, ways = lax.axis_size("tok"), lax.axis_size("vocab")
    left = [("vocab", b) for b in reversed(range(bits_of(ways)))]
    left += [("tok", b) for b in reversed(range(bits_of(groups)))]
    rows = value.shape[0] // (groups * ways)
    return left, value.reshape((2,) * len(left) + (rows, value.shape[1]))


def halves_of(total, left, key):
    at = left.index(key)
    bit = (lax.axis_index(key[0]) >> key[1]) & 1
    away = lax.dynamic_index_in_dim(total, 1 - bit, at, False).astype(jnp.float16)
    return away, lax.dynamic_index_in_dim(total, bit, at, False).astype(jnp.float32)


def per_device(
    teacher_hidden, teacher_head, student_hidden, student_head, grammar_bits, sampled_ids
):
    groups = lax.axis_size("tok")
    mine = lax.axis_index("tok")
    place = lax.axis_index("vocab")
    token_total = student_hidden.shape[0]
    columns = student_head.shape[1]
    start = (place * groups + mine) * columns
    tile = 256
    half = columns // 2

    def product(target, lower, dtype, extras=()):
        return chunk_product(
            teacher_hidden, teacher_head, target * columns + lower, half, tile, dtype, extras
        )

    far, near = [], []
    for lower in (0, half):
        away = product(mine ^ 3, lower, jnp.float32)
        far.append(swapped(away, "tok", 0))
    sent = []
    for at, lower in enumerate((0, half)):
        away = product(mine ^ 2, lower, jnp.float32, (far[at],)).astype(jnp.float16)
        away, mine, student_hidden = lax.optimization_barrier((away, mine, student_hidden))
        sent.append(swapped(away, "tok", 1))
    for lower in (0, half):
        away = product(mine ^ 1, lower, jnp.float32)
        near.append(swapped(away, "tok", 0))
    own = [product(mine, lower, jnp.float32, (near[at],)) for at, lower in enumerate((0, half))]

    student_logit = jnp.dot(student_hidden, student_head, preferred_element_type=jnp.float32)
    student_top = jnp.max(student_logit, axis=1)
    student_sum = jnp.sum(jnp.exp(student_logit - student_top[:, None]), axis=1)
    bit = admitted(words_here(grammar_bits, columns // 16), columns)
    here = start + jnp.arange(columns, dtype=jnp.int32)
    chosen = here[None, :] == sampled_ids[:, None]
    penalty = jnp.where((bit == 1) | chosen, 0.0, -1e30).astype(jnp.bfloat16)

    teacher_logit = jnp.concatenate(
        [own[at] + sent[at].astype(jnp.float32) for at in range(2)], axis=1
    )
    masked = jnp.where(penalty < 0, -1e30, teacher_logit)
    top = jnp.max(masked, axis=1)
    shifted = masked - top[:, None]
    weight = jnp.where(penalty < 0, 0.0, jnp.exp(shifted))
    weight_sum = jnp.sum(weight, axis=1)
    cross = jnp.sum(
        jnp.where(
            penalty < 0, 0.0, weight * (shifted - (student_logit - student_top[:, None]))
        ),
        axis=1,
    )
    picked = jnp.sum(jnp.where(chosen, student_logit - masked, 0.0), axis=1)
    zero = jnp.zeros_like(top)
    part = jnp.stack([top, weight_sum, cross, student_top, student_sum, picked, zero, zero])
    merged = merged_stats(part)
    teacher_top, teacher_sum, cross, student_top, student_sum, picked = (
        merged[i] for i in range(6)
    )
    teacher_lse = jnp.log(teacher_sum)
    student_lse = jnp.log(student_sum)
    divergence = cross / teacher_sum - teacher_lse + student_lse
    gap = picked + (teacher_top - student_top) + (teacher_lse - student_lse)
    distill_loss = jnp.sum(divergence + sample_weight * gap) / token_total

    prob = jnp.where(
        penalty < 0, 0.0, jnp.exp(masked - teacher_top[:, None]) / teacher_sum[:, None]
    ).astype(jnp.bfloat16)
    student_log = student_logit - student_top[:, None] - student_lse[:, None]
    logit_grad = (
        (1.0 - sample_weight) * jnp.exp(student_log)
        - prob.astype(jnp.float32)
        + sample_weight * chosen.astype(jnp.float32)
    ).astype(jnp.bfloat16)

    tok_bits = [("tok", b) for b in range(bits_of(groups))]
    vocab_bits = [("vocab", b) for b in range(bits_of(lax.axis_size("vocab")))]
    orders = (
        tok_bits + vocab_bits,
        tok_bits[:1] + vocab_bits[:1] + tok_bits[1:] + vocab_bits[1:],
    )
    width = student_head.shape[0] // 2
    blocks = []
    for at in range(2):
        block = lax.dot_general(
            logit_grad,
            lax.slice_in_dim(student_head, at * width, (at + 1) * width, axis=0),
            (((1,), (1,)), ((), ())),
            preferred_element_type=jnp.float32,
        )
        blocks.append(block * grad_scale)
    step_rows = 512 if student_hidden.shape[1] % 512 == 0 else 128
    steps = student_hidden.shape[1] // step_rows
    levels = len(orders[0])
    shares = [2, 3, 1, 1] + [0] * levels
    head_grad = None
    step = 0
    lefts, totals = zip(*[split_rows(block) for block in blocks])
    for level in range(levels):
        aways, keeps = [], []
        for at in range(2):
            away, keep = halves_of(totals[at], lefts[at], orders[at][level])
            aways.append(away)
            keeps.append(keep)
        *aways, logit_grad = lax.optimization_barrier((*aways, logit_grad))
        got = [swapped(aways[at], *orders[at][level]) for at in range(2)]
        until = steps if level == levels - 1 else min(steps, step + shares[level])
        if until > step:
            while step < until:
                head_grad = grad_rows(student_hidden, logit_grad, head_grad, step, step_rows)
                step += 1
            *got, head_grad = lax.optimization_barrier((*got, head_grad))
        totals = [keeps[at] + got[at].astype(jnp.float32) for at in range(2)]
        for at in range(2):
            lefts[at].remove(orders[at][level])
    hidden_grad = jnp.concatenate(totals, axis=1) * (1.0 / grad_scale)
    return (distill_loss, head_grad, hidden_grad)


def solution(mesh):
    placed = (
        P(None, "tok"),
        P("tok", "vocab"),
        P(),
        P(None, ("vocab", "tok")),
        P("tok", "vocab"),
        P(),
    )
    return jax.shard_map(
        per_device,
        mesh=mesh,
        in_specs=placed,
        out_specs=(P(), P(None, ("vocab", "tok")), P(("vocab", "tok"), None)),
        check_vma=False,
    )
```

```python
import functools

import jax
import jax.numpy as jnp
from jax import lax
from jax.experimental import pallas as pl
from jax.experimental.pallas import tpu as pltpu
from jax.sharding import PartitionSpec as P

sample_weight = 0.5
grad_scale = 4096.0
MESH = pl.DeviceIdType.MESH


def bits_of(size):
    return size.bit_length() - 1


def swapped(value, axis, bit):
    size = lax.axis_size(axis)
    return lax.ppermute(value, axis, [(i, i ^ (1 << bit)) for i in range(size)])


def chunk_kernel(first_ref, a_ref, b_ref, *rest):
    out_ref = rest[-1]
    total = jnp.dot(a_ref[...], b_ref[...], preferred_element_type=jnp.float32)
    for extra in rest[:-1]:
        total = total + extra[...].astype(jnp.float32)
    out_ref[...] = total.astype(out_ref.dtype)


def chunk_product(a, b, first, width, tile, out_dtype, extras=()):
    rows, depth = a.shape
    tiles = width // tile
    grid_spec = pltpu.PrefetchScalarGridSpec(
        num_scalar_prefetch=1,
        grid=(tiles,),
        in_specs=[
            pl.BlockSpec((rows, depth), lambda i, f: (0, 0)),
            pl.BlockSpec((depth, tile), lambda i, f: (0, f[0] + i)),
        ]
        + [pl.BlockSpec((rows, tile), lambda i, f: (0, i)) for _ in extras],
        out_specs=pl.BlockSpec((rows, tile), lambda i, f: (0, i)),
    )
    return pl.pallas_call(
        chunk_kernel,
        grid_spec=grid_spec,
        out_shape=jax.ShapeDtypeStruct((rows, width), out_dtype),
        compiler_params=pltpu.CompilerParams(vmem_limit_bytes=40 * 1024 * 1024),
        cost_estimate=pl.CostEstimate(
            flops=rows * depth * width // 8,
            bytes_accessed=(rows * depth + depth * width + 2 * rows * width) // 8,
            transcendentals=0,
        ),
    )((first // tile).reshape(1).astype(jnp.int32), a, b, *extras)


def grad_kernel(hidden_ref, grad_ref, *rest):
    rest[-1][...] = lax.dot_general(
        hidden_ref[...],
        grad_ref[...],
        (((0,), (0,)), ((), ())),
        preferred_element_type=jnp.float32,
    ).astype(jnp.bfloat16)


def grad_rows(hidden, grad, earlier, step, tile):
    tokens, width = hidden.shape
    columns = grad.shape[1]
    cut = 2 if columns % 256 == 0 else 1
    held = () if earlier is None else (earlier,)
    return pl.pallas_call(
        grad_kernel,
        grid=(cut,),
        in_specs=[
            pl.BlockSpec((tokens, tile), lambda i: (0, step)),
            pl.BlockSpec((tokens, columns // cut), lambda i: (0, i)),
        ]
        + [pl.BlockSpec(memory_space=pl.ANY) for _ in held],
        out_specs=pl.BlockSpec((tile, columns // cut), lambda i: (step, i)),
        out_shape=jax.ShapeDtypeStruct((width, columns), jnp.bfloat16),
        input_output_aliases={2: 0} if held else {},
        compiler_params=pltpu.CompilerParams(vmem_limit_bytes=24 * 1024 * 1024),
        cost_estimate=pl.CostEstimate(
            flops=2 * tokens * tile * columns,
            bytes_accessed=2 * (tokens * tile + tokens * columns + tile * columns),
            transcendentals=0,
        ),
    )(hidden, grad, *held)


def merge_rows(parts):
    teacher_top = jnp.max(parts[:, 0, :], axis=0, keepdims=True)
    student_top = jnp.max(parts[:, 3, :], axis=0, keepdims=True)
    teacher_shift = parts[:, 0, :] - teacher_top
    student_shift = parts[:, 3, :] - student_top
    scale = jnp.exp(teacher_shift)
    teacher_sum = jnp.sum(parts[:, 1, :] * scale, axis=0, keepdims=True)
    cross = jnp.sum(
        scale * (parts[:, 2, :] + parts[:, 1, :] * (teacher_shift - student_shift)),
        axis=0,
        keepdims=True,
    )
    student_sum = jnp.sum(parts[:, 4, :] * jnp.exp(student_shift), axis=0, keepdims=True)
    picked = jnp.sum(parts[:, 5, :], axis=0, keepdims=True)
    return jnp.concatenate(
        [teacher_top, teacher_sum, cross, student_top, student_sum, picked, picked, picked], axis=0
    )


def stats_kernel(
    groups, ways, part_ref, out_ref, tok_ref, vocab_ref, send_a, recv_a, send_b, recv_b
):
    mine = lax.axis_index("tok")
    place = lax.axis_index("vocab")
    barrier = pltpu.get_barrier_semaphore()
    for step in range(1, groups):
        pl.semaphore_signal(
            barrier,
            inc=1,
            device_id=(place, lax.rem(mine + step, groups)),
            device_id_type=MESH,
        )
    for step in range(1, ways):
        pl.semaphore_signal(
            barrier,
            inc=1,
            device_id=(lax.rem(place + step, ways), mine),
            device_id_type=MESH,
        )
    pl.semaphore_wait(barrier, groups + ways - 2)
    tok_ref[0] = part_ref[...]
    copies = []
    for step in range(1, groups):
        copy = pltpu.make_async_remote_copy(
            src_ref=part_ref,
            dst_ref=tok_ref.at[step],
            send_sem=send_a.at[step],
            recv_sem=recv_a.at[step],
            device_id=(place, lax.rem(mine + step, groups)),
            device_id_type=MESH,
        )
        copy.start()
        copies.append(copy)
    for copy in copies:
        copy.wait()
    vocab_ref[0] = merge_rows(tok_ref[...])
    copies = []
    for step in range(1, ways):
        copy = pltpu.make_async_remote_copy(
            src_ref=vocab_ref.at[0],
            dst_ref=vocab_ref.at[step],
            send_sem=send_b.at[step],
            recv_sem=recv_b.at[step],
            device_id=(lax.rem(place + step, ways), mine),
            device_id_type=MESH,
        )
        copy.start()
        copies.append(copy)
    for copy in copies:
        copy.wait()
    out_ref[...] = merge_rows(vocab_ref[...])


def merged_stats(part):
    groups = lax.axis_size("tok")
    ways = lax.axis_size("vocab")
    return pl.pallas_call(
        functools.partial(stats_kernel, groups, ways),
        out_shape=jax.ShapeDtypeStruct(part.shape, jnp.float32),
        in_specs=[pl.BlockSpec(memory_space=pltpu.VMEM)],
        out_specs=pl.BlockSpec(memory_space=pltpu.VMEM),
        scratch_shapes=[
            pltpu.VMEM((groups,) + part.shape, jnp.float32),
            pltpu.VMEM((ways,) + part.shape, jnp.float32),
            pltpu.SemaphoreType.DMA((groups,)),
            pltpu.SemaphoreType.DMA((groups,)),
            pltpu.SemaphoreType.DMA((ways,)),
            pltpu.SemaphoreType.DMA((ways,)),
        ],
        compiler_params=pltpu.CompilerParams(collective_id=0, has_side_effects=True),
    )(part)


def words_here(grammar_bits, width):
    groups = lax.axis_size("tok")
    mine = lax.axis_index("tok")
    pieces = grammar_bits.reshape(grammar_bits.shape[0], groups, width)
    got = [lax.dynamic_index_in_dim(pieces, mine, 1, False)]
    for step in range(1, groups):
        piece = lax.dynamic_index_in_dim(pieces, mine ^ step, 1, False)
        got.append(lax.ppermute(piece, "tok", [(i, i ^ step) for i in range(groups)]))
    stacked = jnp.stack(got)
    return jnp.concatenate(
        [lax.dynamic_index_in_dim(stacked, mine ^ block, 0, False) for block in range(groups)]
    )


def admitted(words, columns):
    width = words.shape[1]
    low = (words & 255).astype(jnp.bfloat16)
    high = jnp.right_shift(words, 8).astype(jnp.bfloat16)
    spread = jnp.arange(columns, dtype=jnp.int32)
    sources = jnp.arange(2 * width, dtype=jnp.int32)
    wanted = spread // 16 + jnp.where(spread % 16 >= 8, width, 0)
    picks = (sources[:, None] == wanted[None, :]).astype(jnp.bfloat16)
    octets = jnp.dot(
        jnp.concatenate([low, high], axis=1), picks, preferred_element_type=jnp.float32
    ).astype(jnp.int32)
    return jnp.right_shift(octets, (spread % 8)[None, :]) & 1


def split_rows(value):
    groups, ways = lax.axis_size("tok"), lax.axis_size("vocab")
    left = [("vocab", b) for b in reversed(range(bits_of(ways)))]
    left += [("tok", b) for b in reversed(range(bits_of(groups)))]
    rows = value.shape[0] // (groups * ways)
    return left, value.reshape((2,) * len(left) + (rows, value.shape[1]))


def halves_of(total, left, key):
    at = left.index(key)
    bit = (lax.axis_index(key[0]) >> key[1]) & 1
    away = lax.dynamic_index_in_dim(total, 1 - bit, at, False).astype(jnp.float16)
    return away, lax.dynamic_index_in_dim(total, bit, at, False).astype(jnp.float32)


def per_device(
    teacher_hidden, teacher_head, student_hidden, student_head, grammar_bits, sampled_ids
):
    groups = lax.axis_size("tok")
    mine = lax.axis_index("tok")
    place = lax.axis_index("vocab")
    token_total = student_hidden.shape[0]
    columns = student_head.shape[1]
    start = (place * groups + mine) * columns
    tile = 256
    half = columns // 2

    def product(target, lower, dtype, extras=()):
        return chunk_product(
            teacher_hidden, teacher_head, target * columns + lower, half, tile, dtype, extras
        )

    far, near = [], []
    for lower in (0, half):
        away = product(mine ^ 3, lower, jnp.float32)
        far.append(swapped(away, "tok", 0))
    sent = []
    for at, lower in enumerate((0, half)):
        away = product(mine ^ 2, lower, jnp.float32, (far[at],)).astype(jnp.float16)
        away, mine, student_hidden, grammar_bits = lax.optimization_barrier(
            (away, mine, student_hidden, grammar_bits)
        )
        sent.append(swapped(away, "tok", 1))
    for lower in (0, half):
        away = product(mine ^ 1, lower, jnp.float32)
        near.append(swapped(away, "tok", 0))
    own = [product(mine, lower, jnp.float32, (near[at],)) for at, lower in enumerate((0, half))]

    student_logit = jnp.dot(student_hidden, student_head, preferred_element_type=jnp.float32)
    student_top = jnp.max(student_logit, axis=1)
    student_sum = jnp.sum(jnp.exp(student_logit - student_top[:, None]), axis=1)
    bit = admitted(words_here(grammar_bits, columns // 16), columns)
    here = start + jnp.arange(columns, dtype=jnp.int32)
    chosen = here[None, :] == sampled_ids[:, None]
    penalty = jnp.where((bit == 1) | chosen, 0.0, -1e30).astype(jnp.bfloat16)

    teacher_logit = jnp.concatenate(
        [own[at] + sent[at].astype(jnp.float32) for at in range(2)], axis=1
    )
    masked = jnp.where(penalty < 0, -1e30, teacher_logit)
    top = jnp.max(masked, axis=1)
    shifted = masked - top[:, None]
    weight = jnp.where(penalty < 0, 0.0, jnp.exp(shifted))
    weight_sum = jnp.sum(weight, axis=1)
    cross = jnp.sum(
        jnp.where(
            penalty < 0, 0.0, weight * (shifted - (student_logit - student_top[:, None]))
        ),
        axis=1,
    )
    picked = jnp.sum(jnp.where(chosen, student_logit - masked, 0.0), axis=1)
    zero = jnp.zeros_like(top)
    part = jnp.stack([top, weight_sum, cross, student_top, student_sum, picked, zero, zero])
    merged = merged_stats(part)
    teacher_top, teacher_sum, cross, student_top, student_sum, picked = (
        merged[i] for i in range(6)
    )
    teacher_lse = jnp.log(teacher_sum)
    student_lse = jnp.log(student_sum)
    divergence = cross / teacher_sum - teacher_lse + student_lse
    gap = picked + (teacher_top - student_top) + (teacher_lse - student_lse)
    distill_loss = jnp.sum(divergence + sample_weight * gap) / token_total

    prob = jnp.where(
        penalty < 0, 0.0, jnp.exp(masked - teacher_top[:, None]) / teacher_sum[:, None]
    ).astype(jnp.bfloat16)
    student_log = student_logit - student_top[:, None] - student_lse[:, None]
    logit_grad = (
        (1.0 - sample_weight) * jnp.exp(student_log)
        - prob.astype(jnp.float32)
        + sample_weight * chosen.astype(jnp.float32)
    ).astype(jnp.bfloat16)

    tok_bits = [("tok", b) for b in range(bits_of(groups))]
    vocab_bits = [("vocab", b) for b in range(bits_of(lax.axis_size("vocab")))]
    orders = (
        tok_bits + vocab_bits,
        tok_bits[:1] + vocab_bits[:1] + tok_bits[1:] + vocab_bits[1:],
    )
    width = student_head.shape[0] // 2
    blocks = []
    for at in range(2):
        block = lax.dot_general(
            logit_grad,
            lax.slice_in_dim(student_head, at * width, (at + 1) * width, axis=0),
            (((1,), (1,)), ((), ())),
            preferred_element_type=jnp.float32,
        )
        blocks.append(block * grad_scale)
    step_rows = 512 if student_hidden.shape[1] % 512 == 0 else 128
    steps = student_hidden.shape[1] // step_rows
    levels = len(orders[0])
    shares = [2, 3, 1, 1] + [0] * levels
    head_grad = None
    step = 0
    lefts, totals = zip(*[split_rows(block) for block in blocks])
    for level in range(levels):
        aways, keeps = [], []
        for at in range(2):
            away, keep = halves_of(totals[at], lefts[at], orders[at][level])
            aways.append(away)
            keeps.append(keep)
        *aways, logit_grad = lax.optimization_barrier((*aways, logit_grad))
        got = [swapped(aways[at], *orders[at][level]) for at in range(2)]
        until = steps if level == levels - 1 else min(steps, step + shares[level])
        if until > step:
            while step < until:
                head_grad = grad_rows(student_hidden, logit_grad, head_grad, step, step_rows)
                step += 1
            *got, head_grad = lax.optimization_barrier((*got, head_grad))
        totals = [keeps[at] + got[at].astype(jnp.float32) for at in range(2)]
        for at in range(2):
            lefts[at].remove(orders[at][level])
    hidden_grad = jnp.concatenate(totals, axis=1) * (1.0 / grad_scale)
    return (distill_loss, head_grad, hidden_grad)


def solution(mesh):
    placed = (
        P(None, "tok"),
        P("tok", "vocab"),
        P(),
        P(None, ("vocab", "tok")),
        P("tok", "vocab"),
        P(),
    )
    return jax.shard_map(
        per_device,
        mesh=mesh,
        in_specs=placed,
        out_specs=(P(), P(None, ("vocab", "tok")), P(("vocab", "tok"), None)),
        check_vma=False,
    )
```
